512 devices in a mesh: outer: 32 (over x_hi, z), inner: 16 (over y, x_lo, core).
Axes of the slice: x: 4 (x_hi: 2, x_lo: 2; x = x_hi * 2 + x_lo), y: 4, z: 16, core: 2. Of those that a mesh axis runs over, the one named last changes fastest.
Arguments:
- queries: bfloat16 [131072, 1024], P(('outer', 'inner')), may hold values from -10 to 10
- keys: bfloat16 [131072, 256], P(('outer', 'inner')), may hold values from -10 to 10
- values: bfloat16 [131072, 256], P(('outer', 'inner')), may hold values from -18 to 18
- pool_fine: float32 [16, 8], replicated, may hold values from -1.5 to 1.5
- pool_coarse: float32 [8, 8], replicated, may hold values from -2 to 2
- gain: float32 [1024], replicated, may hold values from 0.5 to 1.5
Outputs:
- normed: bfloat16 [131072, 1024], P(('outer', 'inner'))
The draws below stay inside these ranges and needn't reach their ends.
All inputs are finite; a program needn't handle non-finite values.
Results may differ from the reference program's by a relative error of at most 0.008.
Values may be sent and summed in bfloat16 or wider, within the bound.
No kernel may reach another device: no remote copies, remote signals or barrier semaphores. Data moves between devices by JAX's collectives and lax.ppermute only.
A program may use at most 64 MiB of HBM per device.

```python
import jax
import jax.numpy as jnp
from jax import lax

HQ = 16
KVH = 4
HD = 64
BLOCK = 512
FINE = 16
RATIO = 8
D = 1024
COARSE = 128
GROUP = 4096
TOKENS = 131072


def joint_draw(key):
    base = jax.random.fold_in(key, 7)
    draw_q, draw_k = jax.random.split(base, 2)
    width_q = HQ * HD
    width_k = KVH * HD
    queries = jnp.clip(jax.random.normal(draw_q, (TOKENS, width_q), jnp.float32), -6.0, 6.0)
    keys = jnp.clip(jax.random.normal(draw_k, (TOKENS, width_k), jnp.float32), -6.0, 6.0)
    return (queries, keys)


def draw_queries(key, part):
    return joint_draw(key)[0].astype(jnp.bfloat16)


def draw_keys(key, part):
    return joint_draw(key)[1].astype(jnp.bfloat16)


def draw_values(key, part):
    base = jax.random.fold_in(key, 11)
    draw_v = jax.random.fold_in(base, 0)
    drawn = jnp.clip(jax.random.normal(draw_v, (TOKENS, KVH * HD), jnp.float32), -6.0, 6.0)
    return drawn.astype(jnp.bfloat16)


def noise(stream_key, extent, width, reach, held_as=jnp.bfloat16):
    entries = jax.random.normal(stream_key, extent, jnp.float32) * width
    return jnp.minimum(jnp.maximum(entries, -reach), reach).astype(held_as)


def setup_inputs(seed: int = 0) -> dict:
    key_list = jax.random.split(jax.random.key(seed), 7)
    return {
        "queries": draw_queries(jax.random.fold_in(key_list[6], 71), 0),
        "keys": draw_keys(jax.random.fold_in(key_list[6], 71), 0),
        "values": draw_values(jax.random.fold_in(key_list[6], 71), 0),
        "pool_fine": noise(key_list[3], (FINE, 2 * KVH), FINE ** -0.5, 1.5, jnp.float32),
        "pool_coarse": noise(key_list[4], (RATIO, 2 * KVH), RATIO ** -0.5, 2.0, jnp.float32),
        "gain": jnp.clip(1.0 + 0.1 * jax.random.normal(key_list[5], (D,), jnp.float32), 0.5, 1.5),
    }


EPSILON = 1e-06
MASKED_SCORE = -1e+30

def summarize(source, pooling, factor):
    amount = source.shape[0] // factor
    shaped = source.astype(jnp.float32).reshape(amount, factor, 2, KVH, HD)
    weights = pooling.astype(jnp.float32).reshape(factor, 2, KVH)
    pooled = jnp.einsum('mjskd,jsk->mskd', shaped, weights, precision=lax.Precision.HIGHEST)
    return pooled.reshape(amount, 2 * KVH * HD).astype(jnp.bfloat16)

def reference(queries, keys, values, pool_fine, pool_coarse, gain):
    paired = jnp.concatenate([keys, values], axis=1)
    fine_all = summarize(paired, pool_fine, FINE)
    coarse_all = summarize(fine_all, pool_coarse, RATIO)
    padded = jnp.pad(paired, ((BLOCK, BLOCK), (0, 0)))
    fine_group = GROUP // FINE
    coarse_pos = jnp.arange(TOKENS // COARSE, dtype=jnp.int32) * COARSE
    kv_width = KVH * HD

    def one_block(block_idx):
        first_row = (block_idx * BLOCK).astype(jnp.int32)
        query_rows = lax.dynamic_slice_in_dim(queries, first_row, BLOCK, 0)
        near = lax.dynamic_slice_in_dim(padded, first_row, 3 * BLOCK, 0)
        near_pos = first_row - BLOCK + jnp.arange(3 * BLOCK, dtype=jnp.int32)
        near_ok = (near_pos >= 0) & (near_pos < TOKENS)
        group_idx = (first_row // GROUP).astype(jnp.int32)
        fine_rows = lax.dynamic_slice_in_dim(fine_all, (group_idx * fine_group).astype(jnp.int32), fine_group, 0)
        fine_pos = group_idx * GROUP + jnp.arange(fine_group, dtype=jnp.int32) * FINE
        fine_ok = jnp.abs(fine_pos // BLOCK - block_idx) > 1
        coarse_ok = (coarse_pos // GROUP != group_idx) & (jnp.abs(coarse_pos // BLOCK - block_idx) > 1)
        keyset = jnp.concatenate([near, fine_rows, coarse_all], axis=0)
        allowed = jnp.concatenate([near_ok, fine_ok, coarse_ok])
        amount = keyset.shape[0]
        key_heads = keyset[:, :kv_width].astype(jnp.float32).reshape(amount, KVH, HD)
        value_heads = keyset[:, kv_width:].astype(jnp.float32).reshape(amount, KVH, HD)
        query_heads = query_rows.astype(jnp.float32).reshape(BLOCK, KVH, HQ // KVH, HD)
        scores = jnp.einsum('qgrd,kgd->grqk', query_heads, key_heads, precision=lax.Precision.HIGHEST) * HD ** (-0.5)
        scores = jnp.where(allowed, scores, MASKED_SCORE)
        peak = lax.optimization_barrier(jnp.max(scores, axis=3, keepdims=True))
        expon = jnp.where(allowed, jnp.exp(scores - peak), 0.0)
        totals = lax.optimization_barrier(jnp.sum(expon, axis=3))
        rounded = lax.optimization_barrier(expon.astype(jnp.bfloat16)).astype(jnp.float32)
        blended = jnp.einsum('grqk,kgd->qgrd', rounded, value_heads, precision=lax.Precision.HIGHEST)
        attended = blended / jnp.transpose(totals, (2, 0, 1))[..., None]
        return attended.reshape(BLOCK, HQ * HD)
    attended = lax.map(one_block, jnp.arange(TOKENS // BLOCK, dtype=jnp.int32)).reshape(TOKENS, HQ * HD)
    rescale = lax.rsqrt(lax.optimization_barrier(jnp.mean(attended * attended, axis=1, keepdims=True)) + EPSILON)
    return (attended * rescale * gain).astype(jnp.bfloat16)
```

```python
import jax
import jax.numpy as jnp
from jax import lax
from jax.experimental import pallas as pl
from jax.experimental.pallas import tpu as pltpu
from jax.sharding import Mesh
from jax.sharding import PartitionSpec as P

HQ = 16
KVH = 4
HD = 64
BLOCK = 512
FINE = 16
RATIO = 8
D = 1024
TOK = 256
HALF = 512
ZN = 16
GROUPS = 32
INNERS = 16
ZROWS = 8
ALL = ("o0", "z", "y", "xl", "c")
OUTER = ("o0", "z")
INNER = ("y", "xl", "c")
EPSILON = 1e-06
VMEM = pltpu.VMEM
SMEM = pltpu.SMEM
F32 = jnp.float32
BF16 = jnp.bfloat16


def params(mebibytes=48):
    return pltpu.CompilerParams(vmem_limit_bytes=int(mebibytes * 1024 * 1024))


def vmem_spec():
    return pl.BlockSpec(memory_space=VMEM)


def smem_spec():
    return pl.BlockSpec(memory_space=SMEM)


def hbm_spec():
    return pl.BlockSpec(memory_space=pltpu.HBM)


def widen(w, part_dim):
    part = lax.broadcasted_iota(jnp.int32, (2 * KVH, 2 * KVH * HD), 0)
    lane = lax.broadcasted_iota(jnp.int32, (2 * KVH, 2 * KVH * HD), 1)
    pick = jnp.where(lane // HD == part, 1.0, 0.0)
    return lax.dot_general(
        w, pick, (((part_dim,), (0,)), ((), ())), precision=lax.Precision.HIGHEST, preferred_element_type=F32
    )


def begin_kernel(
    core_ref, q_hbm, k_hbm, v_hbm, wf_hbm, wc_hbm, fine_ref, coarse_ref, send_ref, qm_ref, kvm_ref, k_s, v_s, wf_s, wc_s, sems
):
    pairs = [(wf_hbm, wf_s), (wc_hbm, wc_s), (k_hbm, k_s), (v_hbm, v_s)]
    mine = core_ref[0]
    for src, width, at in ((q_hbm, HALF, 256), (k_hbm, 128, 0), (v_hbm, 128, 128)):
        for which, dst in ((1 - mine, send_ref), (mine, kvm_ref if width == 128 else qm_ref)):
            cols = pl.ds(pl.multiple_of(which * width, 128), width)
            start = 0 if dst is qm_ref else at
            pairs.append((src.at[:, cols], dst.at[:, start : start + width]))
    copies = [pltpu.make_async_copy(src, dst, sems.at[i]) for i, (src, dst) in enumerate(pairs)]
    for copy in copies:
        copy.start()
    copies[0].wait()
    copies[1].wait()
    wf = widen(wf_s[...], 0)
    wc = widen(wc_s[...], 1)
    if ZROWS > 8:
        coarse_ref[:, 8:, :] = jnp.zeros((GROUPS, ZROWS - 8, 128), BF16)
    for kv in range(2):
        copies[2 + kv].wait()
        cols = slice(kv * 256, (kv + 1) * 256)
        x = (k_s, v_s)[kv][...].astype(F32).reshape(TOK // FINE, FINE, 256)
        fine = jnp.sum(x * wf[None, :, cols], axis=1).astype(BF16)
        f = fine.astype(F32).reshape(2, RATIO, 256)
        coarse = jnp.sum(f * wc[None, :, cols], axis=1)
        for i in range(2):
            part = 2 * kv + i
            fine_ref[part] = fine[:, i * 128 : (i + 1) * 128]
            rows = jnp.broadcast_to(coarse[None, :, i * 128 : (i + 1) * 128], (GROUPS, 2, 128))
            coarse_ref[:, 2 * part : 2 * part + 2, :] = rows.astype(BF16)
    for copy in copies[4:]:
        copy.wait()


def begin(core, queries, keys, values, pool_fine, pool_coarse):
    return pl.pallas_call(
        begin_kernel,
        out_shape=(
            jax.ShapeDtypeStruct((4, TOK // FINE, 128), BF16),
            jax.ShapeDtypeStruct((GROUPS, ZROWS, 128), BF16),
            jax.ShapeDtypeStruct((TOK, 768), BF16),
            jax.ShapeDtypeStruct((TOK, HALF), BF16),
            jax.ShapeDtypeStruct((TOK, 256), BF16),
        ),
        in_specs=[smem_spec()] + [hbm_spec()] * 5,
        out_specs=(vmem_spec(),) * 5,
        scratch_shapes=[
            VMEM((TOK, 256), BF16),
            VMEM((TOK, 256), BF16),
            VMEM((2 * KVH, FINE), F32),
            VMEM((RATIO, 2 * KVH), F32),
            pltpu.SemaphoreType.DMA((10,)),
        ],
        compiler_params=params(54),
    )(core, queries, keys, values, pool_fine.T, pool_coarse)


NFINE = 256
NCOARSE = 1024
NFAR = NFINE + NCOARSE
LIMIT = 40.0


def cost(keys, times=1):
    return pl.CostEstimate(
        flops=8 * BLOCK * keys * 128 * 4 * times, bytes_accessed=4 << 20, transcendentals=8 * BLOCK * keys
    )


def swapped(x):
    return jnp.concatenate([x[:, 64:], x[:, :64]], axis=1)


def is_low(rows):
    return lax.broadcasted_iota(jnp.int32, (rows, 128), 1) < 64


def scores_of(q, k):
    return lax.dot_general(q, k, (((1,), (1,)), ((), ())), preferred_element_type=F32)


def first_lane(rows, keep=None):
    one = lax.broadcasted_iota(jnp.int32, (rows, 128), 1) == 0
    if keep is not None:
        one = one & keep
    return jnp.where(one, 1.0, 0.0).astype(BF16)


def fine_keep(group, block):
    row = lax.broadcasted_iota(jnp.int32, (NFINE, 128), 0)
    src_block = group * 8 + row // 32
    return jnp.abs(src_block - block) > 1


def coarse_keep(group, block):
    row = lax.broadcasted_iota(jnp.int32, (NCOARSE, 128), 0)
    src_group = (row // 2) % GROUPS
    src_block = src_group * 8 + row // 128
    return (src_group != group) & (jnp.abs(src_block - block) > 1)


def prep_kernel(place_ref, qm_ref, got_ref, q_ref, keep_ref):
    group = place_ref[0]
    block = place_ref[1]
    keep_ref[0:NFINE, :] = jnp.where(fine_keep(group, block), 1.0, 0.0).astype(BF16)
    keep_ref[NFINE:, :] = jnp.where(coarse_keep(group, block), 1.0, 0.0).astype(BF16)
    low = is_low(TOK)
    for ref, first, at in ((qm_ref, 0, 0), (got_ref, 256, TOK)):
        pairs = [ref[:, first + j * 128 : first + (j + 1) * 128].astype(F32) * HD ** (-0.5) for j in range(4)]
        other = [swapped(x) for x in pairs]
        for j in range(2):
            rows = slice(at, at + TOK)
            q_ref[2 * j, rows, :] = jnp.where(low, pairs[j], other[j + 2]).astype(BF16)
            q_ref[2 * j + 1, rows, :] = jnp.where(low, other[j], pairs[j + 2]).astype(BF16)


def prep(place, qm, got):
    return pl.pallas_call(
        prep_kernel,
        out_shape=(
            jax.ShapeDtypeStruct((4, BLOCK, 128), BF16),
            jax.ShapeDtypeStruct((NFAR, 128), BF16),
        ),
        in_specs=[smem_spec()] + [vmem_spec()] * 2,
        out_specs=(vmem_spec(), vmem_spec()),
        compiler_params=params(),
        cost_estimate=cost(3 * BLOCK),
    )(place, qm, got)


def of_head(pair, g, low):
    zero = jnp.zeros_like(pair)
    return jnp.where(low, pair, zero) if g == 0 else jnp.where(low, zero, pair)


def near_kernel(place_ref, kv_ref, prev_ref, next_ref, q_ref, o_out, ml_out, o_s, ml_s, k_s, v_s, sems):
    k_s[0:BLOCK, :] = kv_ref[:, :128]
    v_s[0:BLOCK, :128] = kv_ref[:, 128:]
    v_s[0:BLOCK, 128:] = first_lane(BLOCK)
    for i, ref in enumerate((prev_ref, next_ref)):
        rows = slice(BLOCK * (i + 1), BLOCK * (i + 2))
        valid = place_ref[2 + i] > 0

        @pl.when(valid)
        def _(ref=ref, rows=rows):
            k_s[rows, :] = ref[:, :128]
            v_s[rows, :128] = ref[:, 128:]
            v_s[rows, 128:] = first_lane(BLOCK)

        @pl.when(jnp.logical_not(valid))
        def _(rows=rows):
            k_s[rows, :] = k_s[0:BLOCK, :]
            v_s[rows, :] = jnp.zeros((BLOCK, 256), BF16)

    low = is_low(TOK)
    lane = lax.broadcasted_iota(jnp.int32, (TOK, 128), 1)
    copies = []
    sides = [jnp.zeros((TOK, 128), F32)] * 2
    for i in range(4):
        for t in range(2):
            rows = slice(t * TOK, (t + 1) * TOK)
            outs = []
            for g in range(2):
                h = 4 * g + i
                s = scores_of(of_head(q_ref[i, rows, :], g, low), k_s[...])
                m = jnp.max(s, axis=1, keepdims=True)
                p = jnp.exp(s - m).astype(BF16)
                o = jnp.dot(p, v_s[...], preferred_element_type=F32)
                outs.append(o[:, :128])
                sides[t] = jnp.where(lane == 2 * h, o[:, 128:129], jnp.where(lane == 2 * h + 1, m, sides[t]))
            o_s[i, rows, :] = jnp.where(low, outs[0], outs[1])
        copies.append(pltpu.make_async_copy(o_s.at[i], o_out.at[i], sems.at[i]))
        copies[-1].start()
    for t in range(2):
        ml_s[t * TOK : (t + 1) * TOK, :] = sides[t]
    copies.append(pltpu.make_async_copy(ml_s, ml_out, sems.at[4]))
    copies[-1].start()
    for copy in copies:
        copy.wait()


def near(place, kv, prev, nxt, q):
    return pl.pallas_call(
        near_kernel,
        out_shape=(
            jax.ShapeDtypeStruct((4, BLOCK, 128), F32),
            jax.ShapeDtypeStruct((BLOCK, 128), F32),
        ),
        in_specs=[smem_spec()] + [vmem_spec()] * 4,
        out_specs=(hbm_spec(),) * 2,
        scratch_shapes=[
            VMEM((4, BLOCK, 128), F32),
            VMEM((BLOCK, 128), F32),
            VMEM((3 * BLOCK, 128), BF16),
            VMEM((3 * BLOCK, 256), BF16),
            pltpu.SemaphoreType.DMA((5,)),
        ],
        compiler_params=params(52.5),
        cost_estimate=cost(3 * BLOCK, 8),
    )(place, kv, prev, nxt, q)


def far_kernel(
    got_ref, o_hbm, ml_hbm, q_hbm, keep_hbm, mine_ref, theirs_ref,
    o_s, ml_s, q_s, keep_ref, y_s, k_s, v_s, peak_s, sems,
):
    keep_copy = pltpu.make_async_copy(keep_hbm, keep_ref, sems.at[0])
    ml_copy = pltpu.make_async_copy(ml_hbm, ml_s, sems.at[1])
    q_copies = [pltpu.make_async_copy(q_hbm.at[i], q_s.at[i], sems.at[2 + i]) for i in range(4)]
    o_copies = [pltpu.make_async_copy(o_hbm.at[i], o_s.at[i], sems.at[6 + i]) for i in range(4)]
    for copy in [keep_copy, q_copies[0], ml_copy, o_copies[0]] + q_copies[1:] + o_copies[1:]:
        copy.start()
    k_s[0:NFINE, :] = got_ref[:, 0, 64:80].reshape(NFINE, 128)
    k_s[NFINE:, :] = got_ref[:, 0, 0:64].reshape(NCOARSE, 128)
    keep_copy.wait()
    keep = keep_ref[...]
    v_s[0:NFINE, :128] = got_ref[:, 1, 64:80].reshape(NFINE, 128) * keep[0:NFINE]
    v_s[NFINE:, :128] = got_ref[:, 1, 0:64].reshape(NCOARSE, 128) * keep[NFINE:]
    v_s[:, 128:] = first_lane(NFAR) * keep
    ml_copy.wait()
    low = is_low(TOK)
    top = jnp.full((8, 128), -1e30, F32)
    for i in range(4):
        q_copies[i].wait()
        o_copies[i].wait()
        for t in range(2):
            rows = slice(t * TOK, (t + 1) * TOK)
            outs = []
            for g in range(2):
                h = 4 * g + i
                m = ml_s[rows, 2 * h + 1 : 2 * h + 2]
                d = scores_of(of_head(q_s[i, rows, :], g, low), k_s[...]) - m
                tile = jnp.max(d.reshape(TOK // 8, 8, NFAR), axis=0)
                top = jnp.maximum(top, jnp.max(tile.reshape(8, NFAR // 128, 128), axis=1))
                p = jnp.exp(d).astype(BF16)
                o = jnp.dot(p, v_s[...], preferred_element_type=F32)
                total = o[:, 128:129] + ml_s[rows, 2 * h : 2 * h + 1]
                outs.append((o[:, :128] + o_s[i, rows, :]) * (1.0 / total))
            y_s[i, rows, :] = jnp.where(low, outs[0], outs[1])
    peak_s[...] = top

    @pl.when(jnp.max(peak_s[...]) > LIMIT)
    def _():
        for i in range(4):

            @pl.loop(0, BLOCK // 64)
            def _(t, i=i):
                rows = pl.ds(pl.multiple_of(t * 64, 64), 64)
                low = is_low(64)
                counted = scores_of(jnp.ones((64, 128), BF16), v_s[:, 128:]) > 0
                outs = []
                for g in range(2):
                    h = 4 * g + i
                    s = scores_of(of_head(q_s[i, rows, :], g, low), k_s[...])
                    s = jnp.where(counted, s, -1e30)
                    old = ml_s[rows, 2 * h + 1 : 2 * h + 2]
                    m = jnp.maximum(jnp.max(s, axis=1, keepdims=True), old)
                    p = jnp.exp(s - m).astype(BF16)
                    o = jnp.dot(p, v_s[...], preferred_element_type=F32)
                    shrink = jnp.exp(old - m)
                    total = o[:, 128:129] + ml_s[rows, 2 * h : 2 * h + 1] * shrink
                    outs.append((o[:, :128] + o_s[i, rows, :] * shrink) * (1.0 / total))
                y_s[i, rows, :] = jnp.where(low, outs[0], outs[1])

    for ref, at in ((mine_ref, 0), (theirs_ref, TOK)):
        y = [y_s[i, at : at + TOK, :] for i in range(4)]
        for j in range(2):
            left = jnp.where(low, y[2 * j], swapped(y[2 * j + 1]))
            right = jnp.where(low, swapped(y[2 * j]), y[2 * j + 1])
            ref[:, j * 128 : (j + 1) * 128] = left.astype(BF16)
            ref[:, (j + 2) * 128 : (j + 3) * 128] = right.astype(BF16)


def far(got, o, ml, q, keep):
    return pl.pallas_call(
        far_kernel,
        out_shape=(jax.ShapeDtypeStruct((TOK, HALF), BF16),) * 2,
        in_specs=[vmem_spec()] + [hbm_spec()] * 4,
        out_specs=(vmem_spec(),) * 2,
        scratch_shapes=[
            VMEM((4, BLOCK, 128), F32),
            VMEM((BLOCK, 128), F32),
            VMEM((4, BLOCK, 128), BF16),
            VMEM((NFAR, 128), BF16),
            VMEM((4, BLOCK, 128), F32),
            VMEM((NFAR, 128), BF16),
            VMEM((NFAR, 256), BF16),
            VMEM((8, 128), F32),
            pltpu.SemaphoreType.DMA((10,)),
        ],
        compiler_params=params(51),
        cost_estimate=cost(NFAR),
    )(got, o, ml, q, keep)


def pack_kernel(z_ref, fine_ref, out_ref):
    row = lax.broadcasted_iota(jnp.int32, (256, 256), 0)
    col = lax.broadcasted_iota(jnp.int32, (256, 256), 1)
    part = ((row // 64) % 2) * 2 + row // 128
    source = ((row % 64) // 2) * 8 + part * 2 + row % 2
    pick = jnp.where(col == source, 1.0, 0.0).astype(BF16)
    rows = jnp.dot(pick, z_ref[...].reshape(256, 128), preferred_element_type=F32).astype(BF16)
    for core in range(2):
        for kv in range(2):
            at = core * 128 + kv * 64
            both = jnp.concatenate([rows[at : at + 64], fine_ref[kv * 2 + core]], axis=0)
            for chip in range(8):
                out_ref[chip * 2 + core, kv] = both


def pack(z_rows, fine):
    return pl.pallas_call(
        pack_kernel,
        out_shape=jax.ShapeDtypeStruct((INNERS, 2, 80, 128), BF16),
        in_specs=[vmem_spec()] * 2,
        out_specs=vmem_spec(),
        compiler_params=params(),
    )(z_rows, fine)


def norm_kernel(core_ref, mine_ref, got_ref, gain_ref, out_ref):
    first = core_ref[0] == 0
    mine = mine_ref[...].astype(F32)
    got = got_ref[...].astype(F32)
    total = jnp.sum(mine * mine, axis=1, keepdims=True) + jnp.sum(got * got, axis=1, keepdims=True)
    scale = lax.rsqrt(total / D + EPSILON)
    left = jnp.where(first, mine, got)
    right = jnp.where(first, got, mine)
    out_ref[:, :HALF] = (left * scale * gain_ref[:, :HALF]).astype(BF16)
    out_ref[:, HALF:] = (right * scale * gain_ref[:, HALF:]).astype(BF16)


def finish(core, mine, got, gain):
    return pl.pallas_call(
        norm_kernel,
        out_shape=jax.ShapeDtypeStruct((TOK, D), BF16),
        in_specs=[smem_spec()] + [vmem_spec()] * 3,
        out_specs=vmem_spec(),
        compiler_params=params(),
    )(core, mine, got, gain)


def local(queries, keys, values, pool_fine, pool_coarse, gain):
    core = lax.axis_index("c").reshape(1).astype(jnp.int32)
    group = lax.axis_index(("o0", "z"))
    block = group * 8 + lax.axis_index(("y", "xl"))
    n_blocks = lax.axis_size(ALL) // 2
    place = jnp.stack([group, block, block > 0, block < n_blocks - 1]).astype(jnp.int32)
    fine, coarse, send, qm, kvm = begin(core, queries, keys, values, pool_fine, pool_coarse)
    z_rows = lax.all_to_all(coarse, OUTER, split_axis=0, concat_axis=0, tiled=True)

    got = lax.ppermute(send, "c", [(0, 1), (1, 0)])
    kv = jnp.concatenate([kvm, got[:, :256]], axis=0)
    n = 512
    prev = lax.ppermute(kv, ALL, [(i, i + 2) for i in range(n - 2)])
    nxt = lax.ppermute(kv, ALL, [(i + 2, i) for i in range(n - 2)])
    q, keep = prep(place, qm, got)
    z_rows, q, keep = lax.optimization_barrier((z_rows, q, keep))
    plane = pack(z_rows[:, :8], fine)
    summary = lax.all_to_all(plane, INNER, split_axis=0, concat_axis=0, tiled=True)
    o, ml = near(place, kv, prev, nxt, q)
    mine, theirs = far(summary, o, ml, q, keep)
    back = lax.ppermute(theirs, "c", [(0, 1), (1, 0)])
    return finish(core, mine, back, gain.reshape(1, D))


def solution(mesh):
    torus = Mesh(mesh.devices.reshape(2, ZN, 4, 2, 2), ALL)
    spec = P(ALL, None)
    return jax.shard_map(
        local,
        mesh=torus,
        in_specs=(spec, spec, spec, P(), P(), P()),
        out_specs=spec,
        check_vma=False,
    )
```

```python
import jax
import jax.numpy as jnp
from jax import lax
from jax.experimental import pallas as pl
from jax.experimental.pallas import tpu as pltpu
from jax.sharding import Mesh
from jax.sharding import PartitionSpec as P

HQ = 16
KVH = 4
HD = 64
BLOCK = 512
FINE = 16
RATIO = 8
D = 1024
TOK = 256
HALF = 512
ZN = 16
GROUPS = 32
INNERS = 16
ZROWS = 8
ALL = ("o0", "z", "y", "xl", "c")
OUTER = ("o0", "z")
INNER = ("y", "xl", "c")
EPSILON = 1e-06
VMEM = pltpu.VMEM
SMEM = pltpu.SMEM
F32 = jnp.float32
BF16 = jnp.bfloat16


def params(mebibytes=48):
    return pltpu.CompilerParams(vmem_limit_bytes=int(mebibytes * 1024 * 1024))


def vmem_spec():
    return pl.BlockSpec(memory_space=VMEM)


def smem_spec():
    return pl.BlockSpec(memory_space=SMEM)


def hbm_spec():
    return pl.BlockSpec(memory_space=pltpu.HBM)


def widen(w, part_dim):
    part = lax.broadcasted_iota(jnp.int32, (2 * KVH, 2 * KVH * HD), 0)
    lane = lax.broadcasted_iota(jnp.int32, (2 * KVH, 2 * KVH * HD), 1)
    pick = jnp.where(lane // HD == part, 1.0, 0.0)
    return lax.dot_general(
        w, pick, (((part_dim,), (0,)), ((), ())), precision=lax.Precision.HIGHEST, preferred_element_type=F32
    )


def begin_kernel(
    core_ref, q_hbm, k_hbm, v_hbm, wf_hbm, wc_hbm, fine_ref, coarse_ref, send_ref, kvm_ref, k_s, v_s, wf_s, wc_s, sems
):
    pairs = [(wf_hbm, wf_s), (wc_hbm, wc_s), (k_hbm, k_s), (v_hbm, v_s)]
    mine = core_ref[0]
    for src, width, at in ((q_hbm, HALF, 256), (k_hbm, 128, 0), (v_hbm, 128, 128)):
        for which, dst in ((1 - mine, send_ref), (mine, kvm_ref)):
            if width == HALF and dst is kvm_ref:
                continue
            cols = pl.ds(pl.multiple_of(which * width, 128), width)
            pairs.append((src.at[:, cols], dst.at[:, at : at + width]))
    copies = [pltpu.make_async_copy(src, dst, sems.at[i]) for i, (src, dst) in enumerate(pairs)]
    for copy in copies:
        copy.start()
    copies[0].wait()
    copies[1].wait()
    wf = widen(wf_s[...], 0)
    wc = widen(wc_s[...], 1)
    if ZROWS > 8:
        coarse_ref[:, 8:, :] = jnp.zeros((GROUPS, ZROWS - 8, 128), BF16)
    for kv in range(2):
        copies[2 + kv].wait()
        cols = slice(kv * 256, (kv + 1) * 256)
        x = (k_s, v_s)[kv][...].astype(F32).reshape(TOK // FINE, FINE, 256)
        fine = jnp.sum(x * wf[None, :, cols], axis=1).astype(BF16)
        f = fine.astype(F32).reshape(2, RATIO, 256)
        coarse = jnp.sum(f * wc[None, :, cols], axis=1)
        for i in range(2):
            part = 2 * kv + i
            fine_ref[part] = fine[:, i * 128 : (i + 1) * 128]
            rows = jnp.broadcast_to(coarse[None, :, i * 128 : (i + 1) * 128], (GROUPS, 2, 128))
            coarse_ref[:, 2 * part : 2 * part + 2, :] = rows.astype(BF16)
    for copy in copies[4:]:
        copy.wait()


def begin(core, queries, keys, values, pool_fine, pool_coarse):
    return pl.pallas_call(
        begin_kernel,
        out_shape=(
            jax.ShapeDtypeStruct((4, TOK // FINE, 128), BF16),
            jax.ShapeDtypeStruct((GROUPS, ZROWS, 128), BF16),
            jax.ShapeDtypeStruct((TOK, 768), BF16),
            jax.ShapeDtypeStruct((TOK, 256), BF16),
        ),
        in_specs=[smem_spec()] + [hbm_spec()] * 5,
        out_specs=(vmem_spec(),) * 4,
        scratch_shapes=[
            VMEM((TOK, 256), BF16),
            VMEM((TOK, 256), BF16),
            VMEM((2 * KVH, FINE), F32),
            VMEM((RATIO, 2 * KVH), F32),
            pltpu.SemaphoreType.DMA((9,)),
        ],
        compiler_params=params(54),
    )(core, queries, keys, values, pool_fine.T, pool_coarse)


MESSAGE = 80
NFAR = INNERS * MESSAGE
LIMIT = 40.0


def cost(keys, times=1):
    return pl.CostEstimate(
        flops=8 * BLOCK * keys * 128 * 4 * times, bytes_accessed=4 << 20, transcendentals=8 * BLOCK * keys
    )


def swapped(x):
    return jnp.concatenate([x[:, 64:], x[:, :64]], axis=1)


def is_low(rows):
    return lax.broadcasted_iota(jnp.int32, (rows, 128), 1) < 64


def scores_of(q, k):
    return lax.dot_general(q, k, (((1,), (1,)), ((), ())), preferred_element_type=F32)


def first_lane(rows, keep=None):
    one = lax.broadcasted_iota(jnp.int32, (rows, 128), 1) == 0
    if keep is not None:
        one = one & keep
    return jnp.where(one, 1.0, 0.0).astype(BF16)


def counted_rows(group, block):
    source = lax.broadcasted_iota(jnp.int32, (INNERS, MESSAGE, 128), 0)
    row = lax.broadcasted_iota(jnp.int32, (INNERS, MESSAGE, 128), 1)
    coarse = row < 2 * GROUPS
    src_group = jnp.where(coarse, row // 2, group)
    src_block = src_group * 8 + source // 2
    far_off = jnp.abs(src_block - block) > 1
    keep = far_off & (jnp.logical_not(coarse) | (src_group != group))
    return jnp.where(keep, 1.0, 0.0).reshape(NFAR, 128).astype(BF16)


def prep_kernel(place_ref, q_hbm, got_ref, q_ref, qm_ref, sem):
    cols = pl.ds(pl.multiple_of(place_ref[4] * HALF, 128), HALF)
    copy = pltpu.make_async_copy(q_hbm.at[:, cols], qm_ref, sem)
    copy.start()
    low = is_low(TOK)
    for ref, first, at in ((got_ref, 256, TOK), (qm_ref, 0, 0)):
        if ref is qm_ref:
            copy.wait()
        pairs = [ref[:, first + j * 128 : first + (j + 1) * 128].astype(F32) * HD ** (-0.5) for j in range(4)]
        other = [swapped(x) for x in pairs]
        for j in range(2):
            rows = slice(at, at + TOK)
            q_ref[2 * j, rows, :] = jnp.where(low, pairs[j], other[j + 2]).astype(BF16)
            q_ref[2 * j + 1, rows, :] = jnp.where(low, other[j], pairs[j + 2]).astype(BF16)


def prep(place, queries, got):
    return pl.pallas_call(
        prep_kernel,
        out_shape=jax.ShapeDtypeStruct((4, BLOCK, 128), BF16),
        in_specs=[smem_spec(), hbm_spec(), vmem_spec()],
        out_specs=vmem_spec(),
        scratch_shapes=[VMEM((TOK, HALF), BF16), pltpu.SemaphoreType.DMA],
        compiler_params=params(),
        cost_estimate=cost(3 * BLOCK),
    )(place, queries, got)


def of_head(pair, g, low):
    zero = jnp.zeros_like(pair)
    return jnp.where(low, pair, zero) if g == 0 else jnp.where(low, zero, pair)


def near_kernel(place_ref, kv_ref, prev_ref, next_ref, q_ref, o_s, ml_s, k_s, v_s):
    k_s[0:BLOCK, :] = kv_ref[:, :128]
    v_s[0:BLOCK, :128] = kv_ref[:, 128:]
    v_s[0:BLOCK, 128:] = first_lane(BLOCK)
    for i, ref in enumerate((prev_ref, next_ref)):
        rows = slice(BLOCK * (i + 1), BLOCK * (i + 2))
        valid = place_ref[2 + i] > 0

        @pl.when(valid)
        def _(ref=ref, rows=rows):
            k_s[rows, :] = ref[:, :128]
            v_s[rows, :128] = ref[:, 128:]
            v_s[rows, 128:] = first_lane(BLOCK)

        @pl.when(jnp.logical_not(valid))
        def _(rows=rows):
            k_s[rows, :] = k_s[0:BLOCK, :]
            v_s[rows, :] = jnp.zeros((BLOCK, 256), BF16)

    low = is_low(TOK)
    lane = lax.broadcasted_iota(jnp.int32, (TOK, 128), 1)
    sides = [jnp.zeros((TOK, 128), F32)] * 2
    for i in range(4):
        for t in range(2):
            rows = slice(t * TOK, (t + 1) * TOK)
            outs = []
            for g in range(2):
                h = 4 * g + i
                s = scores_of(of_head(q_ref[i, rows, :], g, low), k_s[...])
                m = jnp.max(s, axis=1, keepdims=True)
                p = jnp.exp(s - m).astype(BF16)
                o = jnp.dot(p, v_s[...], preferred_element_type=F32)
                outs.append(o[:, :128])
                sides[t] = jnp.where(lane == 2 * h, o[:, 128:129], jnp.where(lane == 2 * h + 1, m, sides[t]))
            o_s[i, rows, :] = jnp.where(low, outs[0], outs[1]).astype(BF16)
    for t in range(2):
        ml_s[t * TOK : (t + 1) * TOK, :] = sides[t]


def near(place, kv, prev, nxt, q):
    return pl.pallas_call(
        near_kernel,
        out_shape=(
            jax.ShapeDtypeStruct((4, BLOCK, 128), BF16),
            jax.ShapeDtypeStruct((BLOCK, 128), F32),
        ),
        in_specs=[smem_spec()] + [vmem_spec()] * 4,
        out_specs=(vmem_spec(),) * 2,
        scratch_shapes=[
            VMEM((3 * BLOCK, 128), BF16),
            VMEM((3 * BLOCK, 256), BF16),
        ],
        compiler_params=params(48),
        cost_estimate=cost(3 * BLOCK, 8),
    )(place, kv, prev, nxt, q)


def far_kernel(
    place_ref, got_ref, o_s, ml_s, q_s, mine_ref, theirs_ref, y_s, v_s, peak_s
):
    keep = counted_rows(place_ref[0], place_ref[1])
    k = got_ref[:, 0].reshape(NFAR, 128)
    v_s[:, :128] = got_ref[:, 1].reshape(NFAR, 128) * keep
    v_s[:, 128:] = first_lane(NFAR) * keep
    low = is_low(TOK)
    top = jnp.full((8, 128), -1e30, F32)
    for i in range(4):
        for t in range(2):
            rows = slice(t * TOK, (t + 1) * TOK)
            outs = []
            for g in range(2):
                h = 4 * g + i
                m = ml_s[rows, 2 * h + 1 : 2 * h + 2]
                d = scores_of(of_head(q_s[i, rows, :], g, low), k) - m
                tile = jnp.max(d.reshape(TOK // 8, 8, NFAR), axis=0)
                top = jnp.maximum(top, jnp.max(tile.reshape(8, NFAR // 128, 128), axis=1))
                p = jnp.exp(d).astype(BF16)
                o = jnp.dot(p, v_s[...], preferred_element_type=F32)
                total = o[:, 128:129] + ml_s[rows, 2 * h : 2 * h + 1]
                outs.append((o[:, :128], 1.0 / total))
            old = o_s[i, rows, :].astype(F32)
            outs = [(o + old) * scale for o, scale in outs]
            y_s[i, rows, :] = jnp.where(low, outs[0], outs[1])
    peak = top

    @pl.when(jnp.max(peak) > LIMIT)
    def _():
        for i in range(4):

            @pl.loop(0, BLOCK // 64)
            def _(t, i=i):
                rows = pl.ds(pl.multiple_of(t * 64, 64), 64)
                low = is_low(64)
                counted = scores_of(jnp.ones((64, 128), BF16), v_s[:, 128:]) > 0
                outs = []
                for g in range(2):
                    h = 4 * g + i
                    s = scores_of(of_head(q_s[i, rows, :], g, low), k)
                    s = jnp.where(counted, s, -1e30)
                    old = ml_s[rows, 2 * h + 1 : 2 * h + 2]
                    m = jnp.maximum(jnp.max(s, axis=1, keepdims=True), old)
                    p = jnp.exp(s - m).astype(BF16)
                    o = jnp.dot(p, v_s[...], preferred_element_type=F32)
                    shrink = jnp.exp(old - m)
                    total = o[:, 128:129] + ml_s[rows, 2 * h : 2 * h + 1] * shrink
                    outs.append((o[:, :128] + o_s[i, rows, :].astype(F32) * shrink) * (1.0 / total))
                y_s[i, rows, :] = jnp.where(low, outs[0], outs[1])

    for ref, at in ((mine_ref, 0), (theirs_ref, TOK)):
        y = [y_s[i, at : at + TOK, :] for i in range(4)]
        for j in range(2):
            left = jnp.where(low, y[2 * j], swapped(y[2 * j + 1]))
            right = jnp.where(low, swapped(y[2 * j]), y[2 * j + 1])
            ref[:, j * 128 : (j + 1) * 128] = left.astype(BF16)
            ref[:, (j + 2) * 128 : (j + 3) * 128] = right.astype(BF16)


def far(place, got, o, ml, q):
    return pl.pallas_call(
        far_kernel,
        out_shape=(jax.ShapeDtypeStruct((TOK, HALF), BF16),) * 2,
        in_specs=[smem_spec()] + [vmem_spec()] * 4,
        out_specs=(vmem_spec(),) * 2,
        scratch_shapes=[
            VMEM((4, BLOCK, 128), F32),
            VMEM((NFAR, 256), BF16),
            VMEM((8, 128), F32),
        ],
        compiler_params=params(48),
        cost_estimate=cost(NFAR),
    )(place, got, o, ml, q)


def pack_kernel(z_ref, fine_ref, out_ref):
    row = lax.broadcasted_iota(jnp.int32, (256, 256), 0)
    col = lax.broadcasted_iota(jnp.int32, (256, 256), 1)
    part = ((row // 64) % 2) * 2 + row // 128
    source = ((row % 64) // 2) * 8 + part * 2 + row % 2
    pick = jnp.where(col == source, 1.0, 0.0).astype(BF16)
    rows = jnp.dot(pick, z_ref[...].reshape(256, 128), preferred_element_type=F32).astype(BF16)
    for core in range(2):
        for kv in range(2):
            at = core * 128 + kv * 64
            both = jnp.concatenate([rows[at : at + 64], fine_ref[kv * 2 + core]], axis=0)
            for chip in range(8):
                out_ref[chip * 2 + core, kv] = both


def pack(z_rows, fine):
    return pl.pallas_call(
        pack_kernel,
        out_shape=jax.ShapeDtypeStruct((INNERS, 2, 80, 128), BF16),
        in_specs=[vmem_spec()] * 2,
        out_specs=vmem_spec(),
        compiler_params=params(),
    )(z_rows, fine)


def norm_kernel(core_ref, mine_ref, got_ref, gain_ref, out_ref):
    first = core_ref[0] == 0
    mine = mine_ref[...].astype(F32)
    got = got_ref[...].astype(F32)
    total = jnp.sum(mine * mine, axis=1, keepdims=True) + jnp.sum(got * got, axis=1, keepdims=True)
    scale = lax.rsqrt(total / D + EPSILON)
    left = jnp.where(first, mine, got)
    right = jnp.where(first, got, mine)
    out_ref[:, :HALF] = (left * scale * gain_ref[:, :HALF]).astype(BF16)
    out_ref[:, HALF:] = (right * scale * gain_ref[:, HALF:]).astype(BF16)


def finish(core, mine, got, gain):
    return pl.pallas_call(
        norm_kernel,
        out_shape=jax.ShapeDtypeStruct((TOK, D), BF16),
        in_specs=[smem_spec()] + [vmem_spec()] * 3,
        out_specs=vmem_spec(),
        compiler_params=params(),
    )(core, mine, got, gain)


def local(queries, keys, values, pool_fine, pool_coarse, gain):
    core = lax.axis_index("c").reshape(1).astype(jnp.int32)
    group = lax.axis_index(("o0", "z"))
    block = group * 8 + lax.axis_index(("y", "xl"))
    n_blocks = lax.axis_size(ALL) // 2
    place = jnp.stack([group, block, block > 0, block < n_blocks - 1, core[0]]).astype(jnp.int32)
    fine, coarse, send, kvm = begin(core, queries, keys, values, pool_fine, pool_coarse)
    z_rows = lax.all_to_all(coarse, OUTER, split_axis=0, concat_axis=0, tiled=True)

    got = lax.ppermute(send, "c", [(0, 1), (1, 0)])
    kv = jnp.concatenate([kvm, got[:, :256]], axis=0)
    n = 512
    prev = lax.ppermute(kv, ALL, [(i, i + 2) for i in range(n - 2)])
    nxt = lax.ppermute(kv, ALL, [(i + 2, i) for i in range(n - 2)])
    q = prep(place, queries, got)
    z_rows, q = lax.optimization_barrier((z_rows, q))
    plane = pack(z_rows[:, :8], fine)
    summary = lax.all_to_all(plane, INNER, split_axis=0, concat_axis=0, tiled=True)
    o, ml = near(place, kv, prev, nxt, q)
    mine, theirs = far(place, summary, o, ml, q)
    back = lax.ppermute(theirs, "c", [(0, 1), (1, 0)])
    return finish(core, mine, back, gain.reshape(1, D))


def solution(mesh):
    torus = Mesh(mesh.devices.reshape(2, ZN, 4, 2, 2), ALL)
    spec = P(ALL, None)
    return jax.shard_map(
        local,
        mesh=torus,
        in_specs=(spec, spec, spec, P(), P(), P()),
        out_specs=spec,
        check_vma=False,
    )
```

```python
import functools

import jax
import jax.numpy as jnp
from jax import lax
from jax.experimental import pallas as pl
from jax.experimental.pallas import tpu as pltpu
from jax.sharding import Mesh
from jax.sharding import PartitionSpec as P

HQ = 16
KVH = 4
HD = 64
BLOCK = 512
FINE = 16
RATIO = 8
D = 1024
TOK = 256
HALF = 512
ZN = 16
GROUPS = 32
INNERS = 16
ZROWS = 8
ALL = ("o0", "z", "y", "xl", "c")
OUTER = ("o0", "z")
INNER = ("y", "xl", "c")
EPSILON = 1e-06
VMEM = pltpu.VMEM
SMEM = pltpu.SMEM
F32 = jnp.float32
BF16 = jnp.bfloat16


def params(mebibytes=48):
    return pltpu.CompilerParams(vmem_limit_bytes=int(mebibytes * 1024 * 1024))


def vmem_spec():
    return pl.BlockSpec(memory_space=VMEM)


def smem_spec():
    return pl.BlockSpec(memory_space=SMEM)


def hbm_spec():
    return pl.BlockSpec(memory_space=pltpu.HBM)


def widen(w, part_dim):
    part = lax.broadcasted_iota(jnp.int32, (2 * KVH, 2 * KVH * HD), 0)
    lane = lax.broadcasted_iota(jnp.int32, (2 * KVH, 2 * KVH * HD), 1)
    pick = jnp.where(lane // HD == part, 1.0, 0.0)
    return lax.dot_general(
        w, pick, (((part_dim,), (0,)), ((), ())), precision=lax.Precision.HIGHEST, preferred_element_type=F32
    )


def begin_kernel(
    core_ref, q_hbm, k_hbm, v_hbm, wf_hbm, wc_hbm, fine_ref, coarse_ref, send_ref, kvm_ref, k_s, v_s, wf_s, wc_s, sems
):
    pairs = [(wf_hbm, wf_s), (wc_hbm, wc_s), (k_hbm, k_s), (v_hbm, v_s)]
    mine = core_ref[0]
    for src, width, at in ((q_hbm, HALF, 256), (k_hbm, 128, 0), (v_hbm, 128, 128)):
        for which, dst in ((1 - mine, send_ref), (mine, kvm_ref)):
            if width == HALF and dst is kvm_ref:
                continue
            cols = pl.ds(pl.multiple_of(which * width, 128), width)
            pairs.append((src.at[:, cols], dst.at[:, at : at + width]))
    copies = [pltpu.make_async_copy(src, dst, sems.at[i]) for i, (src, dst) in enumerate(pairs)]
    for copy in copies:
        copy.start()
    copies[0].wait()
    copies[1].wait()
    wf = widen(wf_s[...], 0)
    wc = widen(wc_s[...], 1)
    if ZROWS > 8:
        coarse_ref[:, 8:, :] = jnp.zeros((GROUPS, ZROWS - 8, 128), BF16)
    for kv in range(2):
        copies[2 + kv].wait()
        cols = slice(kv * 256, (kv + 1) * 256)
        x = (k_s, v_s)[kv][...].astype(F32).reshape(TOK // FINE, FINE, 256)
        fine = jnp.sum(x * wf[None, :, cols], axis=1).astype(BF16)
        f = fine.astype(F32).reshape(2, RATIO, 256)
        coarse = jnp.sum(f * wc[None, :, cols], axis=1)
        for i in range(2):
            part = 2 * kv + i
            fine_ref[part] = fine[:, i * 128 : (i + 1) * 128]
            rows = jnp.broadcast_to(coarse[None, :, i * 128 : (i + 1) * 128], (GROUPS, 2, 128))
            coarse_ref[:, 2 * part : 2 * part + 2, :] = rows.astype(BF16)
    for copy in copies[4:]:
        copy.wait()


def begin(core, queries, keys, values, pool_fine, pool_coarse):
    return pl.pallas_call(
        begin_kernel,
        out_shape=(
            jax.ShapeDtypeStruct((4, TOK // FINE, 128), BF16),
            jax.ShapeDtypeStruct((GROUPS, ZROWS, 128), BF16),
            jax.ShapeDtypeStruct((TOK, 768), BF16),
            jax.ShapeDtypeStruct((TOK, 256), BF16),
        ),
        in_specs=[smem_spec()] + [hbm_spec()] * 5,
        out_specs=(vmem_spec(),) * 4,
        scratch_shapes=[
            VMEM((TOK, 256), BF16),
            VMEM((TOK, 256), BF16),
            VMEM((2 * KVH, FINE), F32),
            VMEM((RATIO, 2 * KVH), F32),
            pltpu.SemaphoreType.DMA((9,)),
        ],
        compiler_params=params(54),
    )(core, queries, keys, values, pool_fine.T, pool_coarse)


MESSAGE = 80
NFAR = INNERS * MESSAGE
LIMIT = 40.0


def cost(keys, times=1):
    return pl.CostEstimate(
        flops=8 * BLOCK * keys * 128 * 4 * times, bytes_accessed=4 << 20, transcendentals=8 * BLOCK * keys
    )


def swapped(x):
    return jnp.concatenate([x[:, 64:], x[:, :64]], axis=1)


def is_low(rows):
    return lax.broadcasted_iota(jnp.int32, (rows, 128), 1) < 64


def scores_of(q, k):
    return lax.dot_general(q, k, (((1,), (1,)), ((), ())), preferred_element_type=F32)


def first_lane(rows, keep=None):
    one = lax.broadcasted_iota(jnp.int32, (rows, 128), 1) == 0
    if keep is not None:
        one = one & keep
    return jnp.where(one, 1.0, 0.0).astype(BF16)


def counted_rows(group, block):
    source = lax.broadcasted_iota(jnp.int32, (INNERS, MESSAGE, 128), 0)
    row = lax.broadcasted_iota(jnp.int32, (INNERS, MESSAGE, 128), 1)
    coarse = row < 2 * GROUPS
    src_group = jnp.where(coarse, row // 2, group)
    src_block = src_group * 8 + source // 2
    far_off = jnp.abs(src_block - block) > 1
    keep = far_off & (jnp.logical_not(coarse) | (src_group != group))
    return jnp.where(keep, 1.0, 0.0).reshape(NFAR, 128).astype(BF16)


def prep_kernel(place_ref, q_hbm, got_ref, q_ref, qm_ref, sem):
    cols = pl.ds(pl.multiple_of(place_ref[4] * HALF, 128), HALF)
    copy = pltpu.make_async_copy(q_hbm.at[:, cols], qm_ref, sem)
    copy.start()
    low = is_low(TOK)
    for ref, first, at in ((got_ref, 256, TOK), (qm_ref, 0, 0)):
        if ref is qm_ref:
            copy.wait()
        pairs = [ref[:, first + j * 128 : first + (j + 1) * 128].astype(F32) * HD ** (-0.5) for j in range(4)]
        other = [swapped(x) for x in pairs]
        for j in range(2):
            rows = slice(at, at + TOK)
            q_ref[2 * j, rows, :] = jnp.where(low, pairs[j], other[j + 2]).astype(BF16)
            q_ref[2 * j + 1, rows, :] = jnp.where(low, other[j], pairs[j + 2]).astype(BF16)


def prep(place, queries, got):
    return pl.pallas_call(
        prep_kernel,
        out_shape=jax.ShapeDtypeStruct((4, BLOCK, 128), BF16),
        in_specs=[smem_spec(), hbm_spec(), vmem_spec()],
        out_specs=vmem_spec(),
        scratch_shapes=[VMEM((TOK, HALF), BF16), pltpu.SemaphoreType.DMA],
        compiler_params=params(),
        cost_estimate=cost(3 * BLOCK),
    )(place, queries, got)


def of_head(pair, g, low):
    zero = jnp.zeros_like(pair)
    return jnp.where(low, pair, zero) if g == 0 else jnp.where(low, zero, pair)


def near_kernel(place_ref, kv_ref, prev_ref, next_ref, q_ref, o_s, ml_s, k_s, v_s):
    k_s[0:BLOCK, :] = kv_ref[:, :128]
    v_s[0:BLOCK, :128] = kv_ref[:, 128:]
    v_s[0:BLOCK, 128:] = first_lane(BLOCK)
    for i, ref in enumerate((prev_ref, next_ref)):
        rows = slice(BLOCK * (i + 1), BLOCK * (i + 2))
        valid = place_ref[2 + i] > 0

        @pl.when(valid)
        def _(ref=ref, rows=rows):
            k_s[rows, :] = ref[:, :128]
            v_s[rows, :128] = ref[:, 128:]
            v_s[rows, 128:] = first_lane(BLOCK)

        @pl.when(jnp.logical_not(valid))
        def _(rows=rows):
            k_s[rows, :] = k_s[0:BLOCK, :]
            v_s[rows, :] = jnp.zeros((BLOCK, 256), BF16)

    low = is_low(TOK)
    lane = lax.broadcasted_iota(jnp.int32, (TOK, 128), 1)
    sides = [jnp.zeros((TOK, 128), F32)] * 2
    for i in range(4):
        for t in range(2):
            rows = slice(t * TOK, (t + 1) * TOK)
            outs = []
            for g in range(2):
                h = 4 * g + i
                s = scores_of(of_head(q_ref[i, rows, :], g, low), k_s[...])
                m = jnp.max(s, axis=1, keepdims=True)
                p = jnp.exp(s - m).astype(BF16)
                o = jnp.dot(p, v_s[...], preferred_element_type=F32)
                outs.append(o[:, :128])
                sides[t] = jnp.where(lane == 2 * h, o[:, 128:129], jnp.where(lane == 2 * h + 1, m, sides[t]))
            o_s[i, rows, :] = jnp.where(low, outs[0], outs[1]).astype(BF16)
    for t in range(2):
        ml_s[t * TOK : (t + 1) * TOK, :] = sides[t]


def near(place, kv, prev, nxt, q):
    return pl.pallas_call(
        near_kernel,
        out_shape=(
            jax.ShapeDtypeStruct((4, BLOCK, 128), BF16),
            jax.ShapeDtypeStruct((BLOCK, 128), F32),
        ),
        in_specs=[smem_spec()] + [vmem_spec()] * 4,
        out_specs=(vmem_spec(),) * 2,
        scratch_shapes=[
            VMEM((3 * BLOCK, 128), BF16),
            VMEM((3 * BLOCK, 256), BF16),
        ],
        compiler_params=params(48),
        cost_estimate=cost(3 * BLOCK, 8),
    )(place, kv, prev, nxt, q)


def far_kernel(half, place_ref, got_ref, o_s, ml_s, q_s, out_ref, y_s, v_s, peak_s):
    keep = counted_rows(place_ref[0], place_ref[1])
    k = got_ref[:, 0].reshape(NFAR, 128)
    v_s[:, :128] = got_ref[:, 1].reshape(NFAR, 128) * keep
    v_s[:, 128:] = first_lane(NFAR) * keep
    low = is_low(TOK)
    top = jnp.full((8, 128), -1e30, F32)
    for i in range(4):
        for t in (half,):
            rows = slice(t * TOK, (t + 1) * TOK)
            outs = []
            for g in range(2):
                h = 4 * g + i
                m = ml_s[rows, 2 * h + 1 : 2 * h + 2]
                d = scores_of(of_head(q_s[i, rows, :], g, low), k) - m
                tile = jnp.max(d.reshape(TOK // 8, 8, NFAR), axis=0)
                for c in range(NFAR // 128):
                    top = jnp.maximum(top, tile[:, c * 128 : (c + 1) * 128])
                p = jnp.exp(d).astype(BF16)
                o = jnp.dot(p, v_s[...], preferred_element_type=F32)
                total = o[:, 128:129] + ml_s[rows, 2 * h : 2 * h + 1]
                outs.append((o[:, :128], 1.0 / total))
            old = o_s[i, rows, :].astype(F32)
            outs = [(o + old) * scale for o, scale in outs]
            y_s[i, rows, :] = jnp.where(low, outs[0], outs[1])
    peak = top

    @pl.when(jnp.max(peak) > LIMIT)
    def _():
        for i in range(4):

            @pl.loop(half * TOK // 64, (half + 1) * TOK // 64)
            def _(t, i=i):
                rows = pl.ds(pl.multiple_of(t * 64, 64), 64)
                low = is_low(64)
                counted = scores_of(jnp.ones((64, 128), BF16), v_s[:, 128:]) > 0
                outs = []
                for g in range(2):
                    h = 4 * g + i
                    s = scores_of(of_head(q_s[i, rows, :], g, low), k)
                    s = jnp.where(counted, s, -1e30)
                    old = ml_s[rows, 2 * h + 1 : 2 * h + 2]
                    m = jnp.maximum(jnp.max(s, axis=1, keepdims=True), old)
                    p = jnp.exp(s - m).astype(BF16)
                    o = jnp.dot(p, v_s[...], preferred_element_type=F32)
                    shrink = jnp.exp(old - m)
                    total = o[:, 128:129] + ml_s[rows, 2 * h : 2 * h + 1] * shrink
                    outs.append((o[:, :128] + o_s[i, rows, :].astype(F32) * shrink) * (1.0 / total))
                y_s[i, rows, :] = jnp.where(low, outs[0], outs[1])

    for ref, at in ((out_ref, half * TOK),):
        y = [y_s[i, at : at + TOK, :] for i in range(4)]
        for j in range(2):
            left = jnp.where(low, y[2 * j], swapped(y[2 * j + 1]))
            right = jnp.where(low, swapped(y[2 * j]), y[2 * j + 1])
            ref[:, j * 128 : (j + 1) * 128] = left.astype(BF16)
            ref[:, (j + 2) * 128 : (j + 3) * 128] = right.astype(BF16)


def far(half, place, got, o, ml, q):
    return pl.pallas_call(
        functools.partial(far_kernel, half),
        out_shape=jax.ShapeDtypeStruct((TOK, HALF), BF16),
        in_specs=[smem_spec()] + [vmem_spec()] * 4,
        out_specs=vmem_spec(),
        scratch_shapes=[
            VMEM((4, BLOCK, 128), F32),
            VMEM((NFAR, 256), BF16),
            VMEM((8, 128), F32),
        ],
        compiler_params=params(48),
        cost_estimate=cost(NFAR // 2),
    )(place, got, o, ml, q)


def pack_kernel(z_ref, fine_ref, out_ref):
    row = lax.broadcasted_iota(jnp.int32, (256, 256), 0)
    col = lax.broadcasted_iota(jnp.int32, (256, 256), 1)
    part = ((row // 64) % 2) * 2 + row // 128
    source = ((row % 64) // 2) * 8 + part * 2 + row % 2
    pick = jnp.where(col == source, 1.0, 0.0).astype(BF16)
    rows = jnp.dot(pick, z_ref[...].reshape(256, 128), preferred_element_type=F32).astype(BF16)
    for core in range(2):
        for kv in range(2):
            at = core * 128 + kv * 64
            both = jnp.concatenate([rows[at : at + 64], fine_ref[kv * 2 + core]], axis=0)
            for chip in range(8):
                out_ref[chip * 2 + core, kv] = both


def pack(z_rows, fine):
    return pl.pallas_call(
        pack_kernel,
        out_shape=jax.ShapeDtypeStruct((INNERS, 2, 80, 128), BF16),
        in_specs=[vmem_spec()] * 2,
        out_specs=vmem_spec(),
        compiler_params=params(),
    )(z_rows, fine)


def norm_kernel(core_ref, mine_ref, got_ref, gain_ref, out_ref):
    first = core_ref[0] == 0
    mine = mine_ref[...].astype(F32)
    got = got_ref[...].astype(F32)
    total = jnp.sum(mine * mine, axis=1, keepdims=True) + jnp.sum(got * got, axis=1, keepdims=True)
    scale = lax.rsqrt(total / D + EPSILON)
    left = jnp.where(first, mine, got)
    right = jnp.where(first, got, mine)
    out_ref[:, :HALF] = (left * scale * gain_ref[:, :HALF]).astype(BF16)
    out_ref[:, HALF:] = (right * scale * gain_ref[:, HALF:]).astype(BF16)


def finish(core, mine, got, gain):
    return pl.pallas_call(
        norm_kernel,
        out_shape=jax.ShapeDtypeStruct((TOK, D), BF16),
        in_specs=[smem_spec()] + [vmem_spec()] * 3,
        out_specs=vmem_spec(),
        compiler_params=params(),
    )(core, mine, got, gain)


def local(queries, keys, values, pool_fine, pool_coarse, gain):
    core = lax.axis_index("c").reshape(1).astype(jnp.int32)
    group = lax.axis_index(("o0", "z"))
    block = group * 8 + lax.axis_index(("y", "xl"))
    n_blocks = lax.axis_size(ALL) // 2
    place = jnp.stack([group, block, block > 0, block < n_blocks - 1, core[0]]).astype(jnp.int32)
    fine, coarse, send, kvm = begin(core, queries, keys, values, pool_fine, pool_coarse)
    z_rows = lax.all_to_all(coarse, OUTER, split_axis=0, concat_axis=0, tiled=True)

    got = lax.ppermute(send, "c", [(0, 1), (1, 0)])
    kv = jnp.concatenate([kvm, got[:, :256]], axis=0)
    n = 512
    prev = lax.ppermute(kv, ALL, [(i, i + 2) for i in range(n - 2)])
    nxt = lax.ppermute(kv, ALL, [(i + 2, i) for i in range(n - 2)])
    q = prep(place, queries, got)
    z_rows, q = lax.optimization_barrier((z_rows, q))
    plane = pack(z_rows[:, :8], fine)
    summary = lax.all_to_all(plane, INNER, split_axis=0, concat_axis=0, tiled=True)
    o, ml = near(place, kv, prev, nxt, q)
    theirs = far(1, place, summary, o, ml, q)
    back = lax.ppermute(theirs, "c", [(0, 1), (1, 0)])
    mine = far(0, place, summary, o, ml, q)
    return finish(core, mine, back, gain.reshape(1, D))


def solution(mesh):
    torus = Mesh(mesh.devices.reshape(2, ZN, 4, 2, 2), ALL)
    spec = P(ALL, None)
    return jax.shard_map(
        local,
        mesh=torus,
        in_specs=(spec, spec, spec, P(), P(), P()),
        out_specs=spec,
        check_vma=False,
    )
```
